32 devices in a mesh: dp: 16 (over z, x, core), tensor: 2 (over y).
Axes of the slice: x: 2, y: 2, z: 4, core: 2. Of those that a mesh axis runs over, the one named last changes fastest.
Arguments:
- tokens: bfloat16 [8192, 1024], P(('dp', 'tensor')), may hold values from -6 to 6
- gain_attn: float32 [1024], replicated, may hold values from 0.5 to 1.5
- gain_ffn: float32 [1024], replicated, may hold values from 0.5 to 1.5
- w_query: bfloat16 [1024, 1024], P('dp', 'tensor'), may hold values from -0.1875 to 0.1875
- w_key: bfloat16 [1024, 512], P('dp', 'tensor'), may hold values from -0.1875 to 0.1875
- w_value: bfloat16 [1024, 512], P('dp', 'tensor'), may hold values from -0.1875 to 0.1875
- w_out: bfloat16 [1024, 1024], P('tensor', 'dp'), may hold values from -0.75 to 0.75
- w_gate: bfloat16 [32, 1024, 512], P('tensor', 'dp'), may hold values from -0.1875 to 0.1875
- w_up: bfloat16 [32, 1024, 512], P('tensor', 'dp'), may hold values from -0.1875 to 0.1875
- w_down: bfloat16 [32, 512, 1024], P('tensor', None, 'dp'), may hold values from -1 to 1
- route_gates: float32 [8192, 8], P('dp'), may hold values from 0 to 1, as said below
- routes: int32 [8192, 8], P('dp'), may hold values from 0 to 31, all different within a row; in each aligned block of 512 rows (0 to 511, 512 to 1023, ...) at most 160 rows name the same one
- cotangent: bfloat16 [8192, 1024], P(('dp', 'tensor')), may hold values from -6 to 6
Outputs:
- layer_out: bfloat16 [8192, 1024], P(('dp', 'tensor'))
- grad_tokens: float32 [8192, 1024], P(('dp', 'tensor'))
- grad_gates: float32 [8192, 8], P(('dp', 'tensor'))
- grad_gain_attn: float32 [1024], replicated
- grad_gain_ffn: float32 [1024], replicated
- grad_query: float32 [1024, 1024], P('dp', 'tensor')
- grad_key: float32 [1024, 512], P('dp', 'tensor')
- grad_value: float32 [1024, 512], P('dp', 'tensor')
- grad_out: float32 [1024, 1024], P('tensor', 'dp')
- grad_gate: float32 [32, 1024, 512], P('tensor', 'dp')
- grad_up: float32 [32, 1024, 512], P('tensor', 'dp')
- grad_down: float32 [32, 512, 1024], P('tensor', None, 'dp')
The draws below stay inside these ranges and needn't reach their ends.
Inputs may be any that keep to these rules, and one draw needn't show every extreme that they name: `routes`: each row names 8 different experts; among the 512 rows of one index of dp no expert is named by more than 160 rows, a bound that some block reaches. `route_gates`: each row is positive and sums to one.
All inputs are finite; a program needn't handle non-finite values.
Results may differ from the reference program's by a relative error of at most 0.019.
Values may be sent and summed in bfloat16 or wider, within the bound.
A program may use at most 192 MiB of HBM per device.

```python
import math
import jax
import jax.numpy as jnp
import numpy as np
from jax import lax

D = 1024
HEADS = 16
KV_HEADS = 8
HEAD_DIM = 64
EXPERTS = 32
TOP = 8
FF = 512
TOK_GRP = 512
SEQ_LEN = 512
SEQS = 1
TOKENS = 8192
CAP = 160


def draw_route_gates(key, part):
    key = jax.random.fold_in(key, 11)
    logits = 0.5 * jax.random.normal(key, (TOKENS, TOP), jnp.float32)
    return jax.nn.softmax(logits, axis=-1)


def strengthened(entries, own_key, source, target, parts, factor):
    def block_of(dim):
        return (jnp.arange(entries.shape[dim]) // (entries.shape[dim] // parts)).reshape((-1,) + (1,) * (entries.ndim - 1 - dim))

    near = jax.random.permutation(own_key, parts)[block_of(target)]
    other_side = (block_of(target) + parts // 2) % parts
    return jnp.where((block_of(source) == near) | (block_of(source) == other_side), factor * entries, entries)


def level_of(stream_key, dims, split, low, top_value):
    level, own = 1.0, jax.random.fold_in(stream_key, 6)
    for dim, parts in split:
        heights = jnp.exp(jax.random.uniform(jax.random.fold_in(own, dim), (parts,), jnp.float32, low / len(split), top_value / len(split)))
        level = level * jnp.repeat(heights, dims[dim] // parts).reshape([-1 if axis == dim else 1 for axis in range(len(dims))])
    return level


def assign_block(own_key, own, number, rows, number_of, top, bound, lean):
    ranking = jax.random.permutation(own_key, number_of)
    heavy_load, usual = shares(number_of, rows * top, bound, lean, True), shares(number_of, rows * top, bound, lean, False)
    places = jnp.arange(number_of)

    def named(lengths, turn):
        used = int((lengths > 0).sum())
        fixed = max(1, used // 4)
        shifted = fixed + (places - fixed + turn * (used - fixed)) % max(1, number_of - fixed)
        return jnp.zeros((number_of,), jnp.int32).at[ranking[jnp.where(places < fixed, places, shifted)]].set(jnp.asarray(lengths, jnp.int32))

    lengths = jnp.where(number % 4 == 0, named(heavy_load, number // 4), named(usual, number - number // 4 - 1))
    mixed = jax.random.permutation(jax.random.fold_in(own, 3), number_of)
    donor, receiver = mixed[0:number_of // 2 * 2:2], mixed[1:number_of // 2 * 2:2]
    room = jnp.minimum(lengths[donor] - 1, bound - lengths[receiver]) // 2
    room = jnp.where((donor == ranking[0]) | (receiver == ranking[0]) | (lengths[receiver] == 0), 0, jnp.maximum(room, 0))
    shifted = jax.random.randint(jax.random.fold_in(own, 4), (number_of // 2,), 0, 1 << 20) % (room + 1)
    lengths = lengths.at[donor].add(-shifted).at[receiver].add(shifted)
    labels = jnp.searchsorted(jnp.cumsum(lengths), jnp.arange(rows * top), side="right").astype(jnp.int32)
    grid = labels.reshape(top, rows).T
    grid = grid[jax.random.permutation(jax.random.fold_in(own, 1), rows)]
    turn = jax.random.randint(jax.random.fold_in(own, 2), (rows, 1), 0, top)
    return jnp.take_along_axis(grid, (jnp.arange(top)[None, :] + turn) % top, axis=1)


def shares(number_of, total, most, lean, full):
    loads = [(1 << 20) // math.isqrt(grade ** lean) + 1 for grade in range(1, number_of + 1)]
    largest = most if full else min(most, max(-(-total // number_of), total * loads[0] // sum(loads)))
    least = 1 if total - largest >= number_of - 1 else 0
    counts, rest = [largest] + [least] * (number_of - 1), total - largest - least * (number_of - 1)
    while rest > 0:
        candidates = [i for i in range(1, number_of) if counts[i] < largest] or [i for i in range(1, number_of) if counts[i] < most]
        whole, remaining = sum([loads[i] for i in candidates]), rest
        for i in candidates:
            extra = min(most - counts[i], max(1, remaining * loads[i] // whole), rest)
            counts[i] = counts[i] + extra
            rest = rest - extra
    return np.array(counts)


def gaussian(own_key, extent, spread, most, split=(), kind=jnp.bfloat16):
    values = jax.random.normal(own_key, extent, jnp.float32) * spread
    if len(split) > 0:
        values = level_of(own_key, extent, split, -0.22, 0.18) * values
    return jnp.clip(values, min=-most, max=most).astype(kind)


def gaussian_with(rng, dims, scale, reach, cuts, heavy, held_as=jnp.bfloat16):
    values = scale * jax.random.normal(rng, dims, jnp.float32)
    if cuts:
        values = values * level_of(rng, dims, cuts, -0.22, 0.18)
    return jnp.clip(strengthened(values, jax.random.fold_in(rng, 3), *heavy), -reach, reach).astype(held_as)


def setup_inputs(seed: int = 0) -> dict:
    seeds = jax.random.split(jax.random.key(seed), 14)
    tokens = gaussian_with(seeds[0], (TOKENS, D), 1.0, 6.0, ((0, 32),), (0, 1, 32, 2.75))
    gain_attn = jnp.clip(1.0 + 0.1 * jax.random.normal(seeds[1], (D,), jnp.float32), 0.5, 1.5)
    gain_ffn = jnp.clip(1.0 + 0.1 * jax.random.normal(seeds[2], (D,), jnp.float32), 0.5, 1.5)
    w_query = gaussian(seeds[3], (D, HEADS * HEAD_DIM), D ** -0.5, 0.1875, ((0, 16), (1, 2)))
    w_key = gaussian(seeds[4], (D, KV_HEADS * HEAD_DIM), D ** -0.5, 0.1875, ((0, 16), (1, 2)))
    w_value = gaussian(seeds[5], (D, KV_HEADS * HEAD_DIM), D ** -0.5, 0.1875, ((0, 16), (1, 2)))
    w_out = gaussian(seeds[6], (HEADS * HEAD_DIM, D), (HEADS * HEAD_DIM // 16) ** -0.5, 0.75, ((0, 2), (1, 16)))
    w_gate = gaussian(seeds[7], (EXPERTS, D, FF), D ** -0.5, 0.1875, ((0, 2), (1, 16)))
    w_up = gaussian(seeds[8], (EXPERTS, D, FF), D ** -0.5, 0.1875, ((0, 2), (1, 16)))
    w_down = gaussian(seeds[9], (EXPERTS, FF, D), (FF // 16) ** -0.5, 1.0, ((0, 2), (2, 16)))
    route_gates = draw_route_gates(jax.random.fold_in(seeds[13], 71), 0)
    routes_keys = jax.random.split(jax.random.fold_in(seeds[11], 1), TOKENS // TOK_GRP)
    routes_turns = jax.random.permutation(jax.random.fold_in(seeds[11], 3), TOKENS // TOK_GRP)
    routes = jax.vmap(lambda own, number: assign_block(jax.random.fold_in(seeds[11], 2), own, number, TOK_GRP, EXPERTS, TOP, CAP, 1))(routes_keys, routes_turns).reshape((TOKENS, TOP))
    cotangent = gaussian(seeds[12], (TOKENS, D), 1.0, 6.0, ((0, 32),))
    return {"tokens": tokens, "gain_attn": gain_attn, "gain_ffn": gain_ffn, "w_query": w_query, "w_key": w_key, "w_value": w_value, "w_out": w_out, "w_gate": w_gate, "w_up": w_up, "w_down": w_down, "route_gates": route_gates, "routes": routes, "cotangent": cotangent}


@jax.custom_vjp
def low(v):
    return lax.optimization_barrier(v.astype(jnp.bfloat16)).astype(jnp.float32)

@jax.custom_vjp
def low_back(v):
    return v

def low_keep(v):
    return (low(v), None)

def low_pass(kept, grad):
    return (grad,)

def back_keep(v):
    return (v, None)

def back_low(kept, grad):
    return (low(grad),)
low.defvjp(low_keep, low_pass)
low_back.defvjp(back_keep, back_low)
epsilon = 1e-06
rope_base = 10000.0
negative = -1e+30

def rope_tables(count_rows, seq_length):
    positions = (jnp.arange(count_rows, dtype=jnp.int32) % seq_length).astype(jnp.float32)
    freqs = rope_base ** (-(jnp.arange(HEAD_DIM // 2, dtype=jnp.int32).astype(jnp.float32) * 2.0 / HEAD_DIM))
    angles = positions[:, None] * freqs[None, :]
    return (jnp.concatenate([jnp.cos(angles), jnp.cos(angles)], -1), jnp.concatenate([jnp.sin(angles), jnp.sin(angles)], -1))

def rotate(values, cosine, sine_table):
    halfway = values.shape[-1] // 2
    turned = jnp.concatenate([-values[..., halfway:], values[..., :halfway]], -1)
    return values * cosine[:, None, :] + turned * sine_table[:, None, :]

def rms_norm(values, gain_vector):
    factor = lax.rsqrt(lax.optimization_barrier(jnp.mean(values * values, -1, keepdims=True)) + epsilon)
    return values * factor * gain_vector

def dispatch(route_rows, first_expert, expert_count, capacity):
    flat_routes = route_rows.reshape(-1)
    offset_ids = flat_routes - first_expert
    onehot = (offset_ids[:, None] == jnp.arange(expert_count, dtype=jnp.int32)[None, :]).astype(jnp.int32)
    earlier = jnp.cumsum(onehot, 0) - onehot
    slot_index = lax.optimization_barrier(jnp.sum(earlier * onehot, 1))
    owned = (offset_ids >= 0) & (offset_ids < expert_count)
    position = jnp.where(owned, offset_ids * capacity + slot_index, expert_count * capacity)
    numbers = jnp.arange(flat_routes.shape[0], dtype=jnp.int32) + 1
    slot_table = jnp.zeros((expert_count * capacity + 1,), jnp.int32).at[position].set(numbers)[:expert_count * capacity]
    filled = slot_table > 0
    source = jnp.maximum(slot_table - 1, 0)
    return (source // TOP, filled, source)

def attend_sequence(pieces):
    queries, key_rows, value_rows = pieces
    highest = lax.Precision.HIGHEST
    grouped = queries.reshape(SEQ_LEN, KV_HEADS, HEADS // KV_HEADS, HEAD_DIM)
    raw_scores = low_back(jnp.einsum('qgrd,kgd->grqk', grouped, key_rows, precision=highest))
    causal = jnp.arange(SEQ_LEN, dtype=jnp.int32)[None, :] <= jnp.arange(SEQ_LEN, dtype=jnp.int32)[:, None]
    scores = jnp.where(causal, raw_scores * HEAD_DIM ** (-0.5), negative)
    probabilities = low(jax.nn.softmax(scores, axis=-1))
    attended_values = jnp.einsum('grqk,kgd->qgrd', probabilities, value_rows, precision=highest)
    return attended_values.reshape(SEQ_LEN, HEADS * HEAD_DIM)

def group_layer(tokens, gate_rows, params, token_index, filled, source, cosine, sine_table):
    gain_attn, gain_ffn, w_query, w_key, w_value, w_out, w_gate, w_up, w_down = params
    highest = lax.Precision.HIGHEST
    normed = low(rms_norm(tokens, gain_attn))
    query_pre = low_back(jnp.dot(normed, w_query, precision=highest))
    key_pre = low_back(jnp.dot(normed, w_key, precision=highest))
    value_pre = low_back(jnp.dot(normed, w_value, precision=highest))
    queries = low(rotate(query_pre.reshape(TOK_GRP, HEADS, HEAD_DIM), cosine, sine_table))
    key_rows = low(rotate(key_pre.reshape(TOK_GRP, KV_HEADS, HEAD_DIM), cosine, sine_table))
    value_rows = low(value_pre).reshape(TOK_GRP, KV_HEADS, HEAD_DIM)
    attended_values = lax.map(jax.checkpoint(attend_sequence), (queries.reshape(SEQS, SEQ_LEN, HEADS, HEAD_DIM), key_rows.reshape(SEQS, SEQ_LEN, KV_HEADS, HEAD_DIM), value_rows.reshape(SEQS, SEQ_LEN, KV_HEADS, HEAD_DIM)))
    mixed = low_back(low(attended_values.reshape(TOK_GRP, HEADS * HEAD_DIM)))
    attended = tokens + low_back(jnp.dot(mixed, w_out, precision=highest))
    routed = low(rms_norm(attended, gain_ffn))
    mask_rows = filled.astype(jnp.float32)
    expert_in = (routed[token_index] * mask_rows[:, None]).reshape(EXPERTS, CAP, D)
    gate_pre = low_back(jnp.einsum('ecd,edf->ecf', expert_in, w_gate, precision=highest))
    up_pre = low_back(jnp.einsum('ecd,edf->ecf', expert_in, w_up, precision=highest))
    hidden = low(jax.nn.silu(gate_pre) * up_pre)
    expert_out = low_back(jnp.einsum('ecf,efd->ecd', hidden, w_down, precision=highest))
    slot_gate = gate_rows.reshape(-1)[source] * mask_rows
    combined = jnp.zeros((TOK_GRP, D), jnp.float32).at[token_index].add(slot_gate[:, None] * expert_out.reshape(-1, D))
    return attended + low_back(combined)

def reference(tokens, gain_attn, gain_ffn, w_query, w_key, w_value, w_out, w_gate, w_up, w_down, route_gates, routes, cotangent):
    params = tuple((array.astype(jnp.float32) for array in (gain_attn, gain_ffn, w_query, w_key, w_value, w_out, w_gate, w_up, w_down)))
    cosine, sine_table = rope_tables(TOK_GRP, SEQ_LEN)
    groups = TOKENS // TOK_GRP

    def one_group(totals, pieces):
        group_tokens, gate_rows, route_rows, grad_rows = pieces
        token_index, filled, source = dispatch(route_rows, 0, EXPERTS, CAP)

        def forward(inputs, gate_values, weights):
            return group_layer(inputs, gate_values, weights, token_index, filled, source, cosine, sine_table)
        result, pullback = jax.vjp(forward, group_tokens.astype(jnp.float32), gate_rows, params)
        grad_inputs, grad_gate_rows, grad_params = pullback(grad_rows.astype(jnp.float32))
        totals = jax.tree.map(lambda earlier_sum, addend: earlier_sum + addend, totals, grad_params)
        return (totals, (result.astype(jnp.bfloat16), grad_inputs, grad_gate_rows))
    initial = jax.tree.map(jnp.zeros_like, params)
    totals, (outputs, grad_inputs, grad_gate_rows) = lax.scan(one_group, initial, (tokens.reshape(groups, TOK_GRP, D), route_gates.reshape(groups, TOK_GRP, TOP), routes.reshape(groups, TOK_GRP, TOP), cotangent.reshape(groups, TOK_GRP, D)))
    return (outputs.reshape(TOKENS, D), grad_inputs.reshape(TOKENS, D), grad_gate_rows.reshape(TOKENS, TOP), totals[0], totals[1], totals[2], totals[3], totals[4], totals[5], totals[6], totals[7], totals[8])
```

```python
import jax
import jax.numpy as jnp
from jax import lax
from jax.sharding import PartitionSpec as P

D = 1024
HEAD_DIM = 64
EXPERTS = 32
TOP = 8
LEN = 1024


epsilon = 1e-06
rope_base = 10000.0
negative = -1e30


def rope_tables(count_rows, seq_length):
    positions = (jnp.arange(count_rows, dtype=jnp.int32) % seq_length).astype(jnp.float32)
    freqs = rope_base ** (
        -(jnp.arange(HEAD_DIM // 2, dtype=jnp.int32).astype(jnp.float32) * 2.0 / HEAD_DIM)
    )
    angles = positions[:, None] * freqs[None, :]
    return (
        jnp.concatenate([jnp.cos(angles), jnp.cos(angles)], -1),
        jnp.concatenate([jnp.sin(angles), jnp.sin(angles)], -1),
    )


def rotate(values, cosine, sine_table):
    halfway = values.shape[-1] // 2
    turned = jnp.concatenate([-values[..., halfway:], values[..., :halfway]], -1)
    return values * cosine[:, None, :] + turned * sine_table[:, None, :]


def rotate_back(grads, cosine, sine_table):
    halfway = grads.shape[-1] // 2
    shifted = grads * sine_table[:, None, :]
    reverted = jnp.concatenate([shifted[..., halfway:], -shifted[..., :halfway]], -1)
    return grads * cosine[:, None, :] + reverted


def normalize(values, gain_vector):
    factor = lax.rsqrt(jnp.mean(values * values, -1, keepdims=True) + epsilon)
    scaled = values * factor
    return ((scaled * gain_vector).astype(jnp.bfloat16), scaled, factor)


def normalize_back(grad_normed, scaled, factor, gain_vector):
    grad_scaled = grad_normed * gain_vector
    gain_term = jnp.sum(grad_normed * scaled, 0)
    grad_values = factor * (
        grad_scaled - scaled * jnp.mean(grad_scaled * scaled, -1, keepdims=True)
    )
    return (gain_term, grad_values)


def spread(values):
    return lax.all_gather(values, "tensor", axis=0, tiled=True)


def sum_rows(term):
    size = lax.axis_size("tensor")
    own_rows = term.shape[0] // size
    if size != 2:
        return lax.psum_scatter(term, "tensor", scatter_dimension=0, tiled=True)
    index = lax.axis_index("tensor")
    kept = lax.dynamic_slice_in_dim(term, index * own_rows, own_rows, 0)
    sent = lax.dynamic_slice_in_dim(term, (1 - index) * own_rows, own_rows, 0)
    received = lax.ppermute(sent.astype(jnp.bfloat16), "tensor", [(0, 1), (1, 0)])
    return kept + received.astype(jnp.float32)


def dispatch(route_rows, gate_rows, first_expert, expert_count, capacity):
    rows = route_rows.shape[0]
    experts = first_expert + jnp.arange(expert_count, dtype=jnp.int32)
    pairs = route_rows[:, :, None] == experts[None, None, :]
    named = jnp.any(pairs, 1)
    row_gates = jnp.sum(jnp.where(pairs, gate_rows[:, :, None], 0.0), 1)
    order = jnp.arange(rows, dtype=jnp.int32)
    before = (order[None, :] < order[:, None]).astype(jnp.bfloat16)
    rank = jnp.dot(
        before, named.astype(jnp.bfloat16), preferred_element_type=jnp.float32
    ).astype(jnp.int32)
    rank = jnp.where(named, rank, capacity)
    slots = rank[:, :, None] == jnp.arange(capacity, dtype=jnp.int32)[None, None, :]
    return (pairs, row_gates, slots)


def block_scores(block_queries, seq_keys, start_row, block_rows, seq_length):
    raw_scores = jnp.einsum(
        "qgrd,kgd->grqk", block_queries, seq_keys, preferred_element_type=jnp.float32
    )
    query_pos = start_row + jnp.arange(block_rows, dtype=jnp.int32)[:, None]
    key_pos = jnp.arange(seq_length, dtype=jnp.int32)[None, :]
    return jnp.where(key_pos <= query_pos, raw_scores * HEAD_DIM ** (-0.5), negative)


def attend_forward(queries, key_rows, value_rows, seq_length, block_rows):
    row_count = queries.shape[0]
    kv_local = key_rows.shape[1]
    repeat_count = queries.shape[1] // kv_local
    seq_count = row_count // seq_length

    def one_sequence(pieces):
        seq_queries, seq_keys, seq_values = pieces
        out_blocks = []
        lse_blocks = []
        for block_index in range(seq_length // block_rows):
            start_row = block_index * block_rows
            block_queries = seq_queries[start_row : start_row + block_rows]
            scores = block_scores(block_queries, seq_keys, start_row, block_rows, seq_length)
            largest = jnp.max(scores, -1, keepdims=True)
            log_total = largest + jnp.log(jnp.sum(jnp.exp(scores - largest), -1, keepdims=True))
            probabilities = jnp.exp(scores - log_total).astype(jnp.bfloat16)
            block_out = jnp.einsum(
                "grqk,kgd->qgrd", probabilities, seq_values, preferred_element_type=jnp.float32
            )
            out_blocks.append(block_out.reshape(block_rows, -1))
            lse_blocks.append(log_total)
        return (jnp.concatenate(out_blocks, 0), jnp.concatenate(lse_blocks, 2))

    attended_values, log_sums = lax.map(
        one_sequence,
        (
            queries.reshape(seq_count, seq_length, kv_local, repeat_count, HEAD_DIM),
            key_rows.reshape(seq_count, seq_length, kv_local, HEAD_DIM),
            value_rows.reshape(seq_count, seq_length, kv_local, HEAD_DIM),
        ),
    )
    return (attended_values.reshape(row_count, -1), log_sums)


def attend_backward(queries, key_rows, value_rows, grad_mixed, log_sums, seq_length, block_rows):
    row_count = queries.shape[0]
    kv_local = key_rows.shape[1]
    repeat_count = queries.shape[1] // kv_local
    seq_count = row_count // seq_length
    scale = HEAD_DIM ** (-0.5)

    def one_sequence(pieces):
        seq_queries, seq_keys, seq_values, seq_grads, seq_sums = pieces
        grad_keys = jnp.zeros((seq_length, kv_local, HEAD_DIM), jnp.float32)
        grad_values = jnp.zeros((seq_length, kv_local, HEAD_DIM), jnp.float32)
        query_blocks = []
        for block_index in range(seq_length // block_rows):
            start_row = block_index * block_rows
            block_queries = seq_queries[start_row : start_row + block_rows]
            block_grads = seq_grads[start_row : start_row + block_rows]
            block_sums = seq_sums[:, :, start_row : start_row + block_rows]
            scores = block_scores(block_queries, seq_keys, start_row, block_rows, seq_length)
            probabilities = jnp.exp(scores - block_sums)
            rounded = probabilities.astype(jnp.bfloat16)
            grad_probs = jnp.einsum(
                "qgrd,kgd->grqk", block_grads, seq_values, preferred_element_type=jnp.float32
            )
            inner = jnp.sum(probabilities * grad_probs, -1, keepdims=True)
            grad_scores = (scale * probabilities * (grad_probs - inner)).astype(jnp.bfloat16)
            query_blocks.append(
                jnp.einsum(
                    "grqk,kgd->qgrd", grad_scores, seq_keys, preferred_element_type=jnp.float32
                )
            )
            grad_keys = grad_keys + jnp.einsum(
                "grqk,qgrd->kgd", grad_scores, block_queries, preferred_element_type=jnp.float32
            )
            grad_values = grad_values + jnp.einsum(
                "grqk,qgrd->kgd", rounded, block_grads, preferred_element_type=jnp.float32
            )
        return (jnp.concatenate(query_blocks, 0), grad_keys, grad_values)

    grad_queries, grad_keys, grad_values = lax.map(
        one_sequence,
        (
            queries.reshape(seq_count, seq_length, kv_local, repeat_count, HEAD_DIM),
            key_rows.reshape(seq_count, seq_length, kv_local, HEAD_DIM),
            value_rows.reshape(seq_count, seq_length, kv_local, HEAD_DIM),
            grad_mixed.reshape(seq_count, seq_length, kv_local, repeat_count, HEAD_DIM),
            log_sums,
        ),
    )
    return (
        grad_queries.reshape(row_count, kv_local * repeat_count, HEAD_DIM),
        grad_keys.reshape(row_count, kv_local, HEAD_DIM),
        grad_values.reshape(row_count, kv_local * HEAD_DIM),
    )


def on_device(
    tokens,
    gain_attn,
    gain_ffn,
    w_query,
    w_key,
    w_value,
    w_out,
    w_gate,
    w_up,
    w_down,
    route_gates,
    routes,
    cotangent,
):
    tensor_size = lax.axis_size("tensor")
    own_rows = tokens.shape[0]
    group_rows = own_rows * tensor_size
    seq_length = min(LEN, group_rows)
    block_rows = min(512, seq_length)
    capacity = group_rows * TOP * 5 // (4 * EXPERTS)
    local_experts = w_gate.shape[0]
    head_count = w_query.shape[1] // HEAD_DIM
    kv_count = w_key.shape[1] // HEAD_DIM
    query_width = w_query.shape[1]
    key_width = w_key.shape[1]
    pre_width = query_width + 2 * key_width
    rows_shard = w_query.shape[0]
    owns_experts = local_experts == lax.axis_size("dp")
    cosine, sine_table = rope_tables(group_rows, seq_length)
    attn_full = lax.all_gather(
        jnp.concatenate([w_query, w_key, w_value, w_out.T], 1), "dp", axis=0, tiled=True
    )
    pre_full = attn_full[:, :pre_width]
    out_full = attn_full[:, pre_width:]
    expert_stack = jnp.stack([w_gate, w_up, w_down.transpose(0, 2, 1)], 1)
    if owns_experts:
        expert_full = lax.all_to_all(expert_stack, "dp", split_axis=0, concat_axis=0, tiled=True)
        gate_full, up_full, down_full = (
            expert_full[:, index].reshape(1, D, expert_stack.shape[3]) for index in range(3)
        )
    else:
        expert_full = lax.all_gather(expert_stack, "dp", axis=2, tiled=True)
        gate_full, up_full, down_full = (expert_full[:, index] for index in range(3))

    def to_experts(rows):
        if not owns_experts:
            return rows.reshape(local_experts, capacity, D)
        moved = lax.all_to_all(
            rows.reshape(local_experts, capacity, D), "dp", split_axis=0, concat_axis=0, tiled=True
        )
        return moved.reshape(1, local_experts * capacity, D)

    def from_experts(rows):
        if not owns_experts:
            return rows.reshape(-1, D)
        moved = lax.all_to_all(
            rows.reshape(local_experts, capacity, D), "dp", split_axis=0, concat_axis=0, tiled=True
        )
        return moved.reshape(-1, D)

    pairs, row_gates, slots = dispatch(
        routes, route_gates, lax.axis_index("tensor") * local_experts, local_experts, capacity
    )
    slot_rows = slots.reshape(group_rows, -1).astype(jnp.bfloat16)
    gated_rows = (
        jnp.where(slots, row_gates[:, :, None], 0.0).astype(jnp.bfloat16).reshape(group_rows, -1)
    )
    slot_gate = jnp.sum(jnp.where(slots, row_gates[:, :, None], 0.0), 0).reshape(-1)
    grad_full = spread(cotangent)
    grad_slots = jnp.einsum("ts,td->sd", slot_rows, grad_full, preferred_element_type=jnp.float32)
    grad_expert = to_experts((slot_gate[:, None] * grad_slots).astype(jnp.bfloat16))

    token_values = tokens.astype(jnp.float32)
    normed_own, scaled_attn, factor_attn = normalize(token_values, gain_attn)
    normed = spread(normed_own)
    pre = jnp.dot(normed, pre_full, preferred_element_type=jnp.float32)
    query_pre = pre[:, :query_width]
    key_pre = pre[:, query_width : query_width + key_width]
    value_pre = pre[:, query_width + key_width :]
    queries = rotate(
        query_pre.reshape(group_rows, head_count, HEAD_DIM), cosine, sine_table
    ).astype(jnp.bfloat16)
    key_rows = rotate(key_pre.reshape(group_rows, kv_count, HEAD_DIM), cosine, sine_table).astype(
        jnp.bfloat16
    )
    value_rows = value_pre.reshape(group_rows, kv_count, HEAD_DIM).astype(jnp.bfloat16)
    attended_values, log_sums = attend_forward(
        queries, key_rows, value_rows, seq_length, block_rows
    )
    mixed = attended_values.astype(jnp.bfloat16)
    attended = token_values + sum_rows(
        jnp.einsum("tc,dc->td", mixed, out_full, preferred_element_type=jnp.float32)
    )
    routed_own, scaled_ffn, factor_ffn = normalize(attended, gain_ffn)
    routed = spread(routed_own)
    expert_in = to_experts(
        jnp.einsum("ts,td->sd", slot_rows, routed, preferred_element_type=jnp.float32).astype(
            jnp.bfloat16
        )
    )
    gate_pre = jnp.einsum("ecd,edf->ecf", expert_in, gate_full, preferred_element_type=jnp.float32)
    up_pre = jnp.einsum("ecd,edf->ecf", expert_in, up_full, preferred_element_type=jnp.float32)
    sigmoid_gate = jax.nn.sigmoid(gate_pre)
    silu_gate = gate_pre * sigmoid_gate
    hidden = (silu_gate * up_pre).astype(jnp.bfloat16)
    expert_out = from_experts(
        jnp.einsum("ecf,edf->ecd", hidden, down_full, preferred_element_type=jnp.float32).astype(
            jnp.bfloat16
        )
    )
    grad_hidden = jnp.einsum(
        "ecd,edf->ecf", grad_expert, down_full, preferred_element_type=jnp.float32
    )
    grad_gate_pre = (
        grad_hidden * up_pre * sigmoid_gate * (1.0 + gate_pre * (1.0 - sigmoid_gate))
    ).astype(jnp.bfloat16)
    grad_up_pre = (grad_hidden * silu_gate).astype(jnp.bfloat16)
    grad_expert_in = jnp.einsum(
        "ecf,edf->ecd", grad_gate_pre, gate_full, preferred_element_type=jnp.float32
    )
    grad_expert_in = grad_expert_in + jnp.einsum(
        "ecf,edf->ecd", grad_up_pre, up_full, preferred_element_type=jnp.float32
    )
    routed_slots = from_experts(grad_expert_in.astype(jnp.bfloat16))
    grad_stack = jnp.stack(
        [
            jnp.einsum("ecd,ecf->edf", left, right, preferred_element_type=jnp.float32).astype(
                jnp.bfloat16
            )
            for left, right in (
                (expert_in, grad_gate_pre),
                (expert_in, grad_up_pre),
                (grad_expert, hidden),
            )
        ],
        1,
    )
    if owns_experts:
        grad_shards = lax.all_to_all(
            grad_stack.reshape(3, local_experts, rows_shard, -1).transpose(1, 0, 2, 3),
            "dp",
            split_axis=0,
            concat_axis=0,
            tiled=True,
        )
    else:
        grad_shards = lax.psum_scatter(grad_stack, "dp", scatter_dimension=2, tiled=True)
    grad_shards = grad_shards.astype(jnp.float32)
    grad_gate, grad_up = (grad_shards[:, 0], grad_shards[:, 1])
    grad_down = grad_shards[:, 2].transpose(0, 2, 1)

    routed_part = jnp.dot(slot_rows, routed_slots, preferred_element_type=jnp.float32)
    grad_routed = sum_rows(routed_part)
    combined = jnp.dot(gated_rows, expert_out, preferred_element_type=jnp.float32)
    layer_out = (attended + sum_rows(combined)).astype(jnp.bfloat16)
    gate_grad = jnp.sum(grad_slots * expert_out.astype(jnp.float32), -1)
    row_grads = jnp.sum(
        jnp.where(slots, gate_grad.reshape(1, local_experts, capacity), 0.0), -1
    )
    gate_part = jnp.sum(jnp.where(pairs, row_grads[:, None, :], 0.0), -1)
    grad_gates = lax.psum_scatter(gate_part, "tensor", scatter_dimension=0, tiled=True)

    gain_ffn_part, attended_norm = normalize_back(grad_routed, scaled_ffn, factor_ffn, gain_ffn)
    grad_attended = cotangent.astype(jnp.float32) + attended_norm
    grad_branch = spread(grad_attended.astype(jnp.bfloat16))
    grad_out_w = jnp.einsum("td,tc->dc", grad_branch, mixed, preferred_element_type=jnp.float32)
    grad_mixed = jnp.dot(grad_branch, out_full, preferred_element_type=jnp.float32).astype(
        jnp.bfloat16
    )
    grad_queries, grad_keys, grad_values = attend_backward(
        queries, key_rows, value_rows, grad_mixed, log_sums, seq_length, block_rows
    )
    grad_query_pre = (
        rotate_back(grad_queries, cosine, sine_table).astype(jnp.bfloat16).reshape(group_rows, -1)
    )
    grad_key_pre = (
        rotate_back(grad_keys, cosine, sine_table).astype(jnp.bfloat16).reshape(group_rows, -1)
    )
    grad_pre = jnp.concatenate([grad_query_pre, grad_key_pre, grad_values.astype(jnp.bfloat16)], 1)
    grad_pre_w = jnp.einsum("td,tc->dc", normed, grad_pre, preferred_element_type=jnp.float32)
    grad_normed = sum_rows(
        jnp.einsum("tc,dc->td", grad_pre, pre_full, preferred_element_type=jnp.float32)
    )
    gain_attn_part, tokens_norm = normalize_back(grad_normed, scaled_attn, factor_attn, gain_attn)
    grad_tokens = grad_attended + tokens_norm
    gain_parts = lax.all_gather(
        jnp.stack([gain_attn_part, gain_ffn_part]), ("dp", "tensor"), axis=0, tiled=False
    )
    gain_sums = jnp.sum(gain_parts, 0)
    grad_gain_attn, grad_gain_ffn = (gain_sums[0], gain_sums[1])
    attn_shards = lax.psum_scatter(
        jnp.concatenate(
            [grad_pre_w.astype(jnp.bfloat16), grad_out_w.astype(jnp.bfloat16)], 1
        ),
        "dp",
        scatter_dimension=0,
        tiled=True,
    ).astype(jnp.float32)
    grad_query = attn_shards[:, :query_width]
    grad_key = attn_shards[:, query_width : query_width + key_width]
    grad_value = attn_shards[:, query_width + key_width : pre_width]
    grad_out = attn_shards[:, pre_width:].T
    return (
        layer_out,
        grad_tokens,
        grad_gates,
        grad_gain_attn,
        grad_gain_ffn,
        grad_query,
        grad_key,
        grad_value,
        grad_out,
        grad_gate,
        grad_up,
        grad_down,
    )


def solution(mesh):
    in_specs = (
        P(("dp", "tensor"), None),
        P(),
        P(),
        P("dp", "tensor"),
        P("dp", "tensor"),
        P("dp", "tensor"),
        P("tensor", "dp"),
        P("tensor", "dp", None),
        P("tensor", "dp", None),
        P("tensor", None, "dp"),
        P("dp", None),
        P("dp", None),
        P(("dp", "tensor"), None),
    )
    out_specs = (
        P(("dp", "tensor"), None),
        P(("dp", "tensor"), None),
        P(("dp", "tensor"), None),
        P(),
        P(),
        P("dp", "tensor"),
        P("dp", "tensor"),
        P("dp", "tensor"),
        P("tensor", "dp"),
        P("tensor", "dp", None),
        P("tensor", "dp", None),
        P("tensor", None, "dp"),
    )
    return jax.shard_map(
        on_device, mesh=mesh, in_specs=in_specs, out_specs=out_specs, check_vma=False
    )
```

```python
import jax
import jax.numpy as jnp
from jax import lax
from jax.sharding import PartitionSpec as P

D = 1024
HEAD_DIM = 64
EXPERTS = 32
TOP = 8
LEN = 1024


epsilon = 1e-06
rope_base = 10000.0
negative = -1e30


def rope_tables(count_rows, seq_length):
    positions = (jnp.arange(count_rows, dtype=jnp.int32) % seq_length).astype(jnp.float32)
    freqs = rope_base ** (
        -(jnp.arange(HEAD_DIM // 2, dtype=jnp.int32).astype(jnp.float32) * 2.0 / HEAD_DIM)
    )
    angles = positions[:, None] * freqs[None, :]
    return (
        jnp.concatenate([jnp.cos(angles), jnp.cos(angles)], -1),
        jnp.concatenate([jnp.sin(angles), jnp.sin(angles)], -1),
    )


def rotate(values, cosine, sine_table):
    halfway = values.shape[-1] // 2
    turned = jnp.concatenate([-values[..., halfway:], values[..., :halfway]], -1)
    return values * cosine[:, None, :] + turned * sine_table[:, None, :]


def rotate_back(grads, cosine, sine_table):
    halfway = grads.shape[-1] // 2
    shifted = grads * sine_table[:, None, :]
    reverted = jnp.concatenate([shifted[..., halfway:], -shifted[..., :halfway]], -1)
    return grads * cosine[:, None, :] + reverted


def normalize(values, gain_vector):
    factor = lax.rsqrt(jnp.mean(values * values, -1, keepdims=True) + epsilon)
    scaled = values * factor
    return ((scaled * gain_vector).astype(jnp.bfloat16), scaled, factor)


def normalize_back(grad_normed, scaled, factor, gain_vector):
    grad_scaled = grad_normed * gain_vector
    gain_term = jnp.sum(grad_normed * scaled, 0)
    grad_values = factor * (
        grad_scaled - scaled * jnp.mean(grad_scaled * scaled, -1, keepdims=True)
    )
    return (gain_term, grad_values)


def spread(values):
    return lax.all_gather(values, "tensor", axis=0, tiled=True)


def sum_rows(term):
    size = lax.axis_size("tensor")
    own_rows = term.shape[0] // size
    if size != 2:
        return lax.psum_scatter(term, "tensor", scatter_dimension=0, tiled=True)
    index = lax.axis_index("tensor")
    kept = lax.dynamic_slice_in_dim(term, index * own_rows, own_rows, 0)
    sent = lax.dynamic_slice_in_dim(term, (1 - index) * own_rows, own_rows, 0)
    received = lax.ppermute(sent.astype(jnp.bfloat16), "tensor", [(0, 1), (1, 0)])
    return kept + received.astype(jnp.float32)


def dispatch(route_rows, gate_rows, first_expert, expert_count, capacity):
    rows = route_rows.shape[0]
    experts = first_expert + jnp.arange(expert_count, dtype=jnp.int32)
    pairs = route_rows[:, :, None] == experts[None, None, :]
    named = jnp.any(pairs, 1)
    row_gates = jnp.sum(jnp.where(pairs, gate_rows[:, :, None], 0.0), 1)
    order = jnp.arange(rows, dtype=jnp.int32)
    before = (order[None, :] < order[:, None]).astype(jnp.bfloat16)
    rank = jnp.dot(
        before, named.astype(jnp.bfloat16), preferred_element_type=jnp.float32
    ).astype(jnp.int32)
    rank = jnp.where(named, rank, capacity)
    slots = rank[:, :, None] == jnp.arange(capacity, dtype=jnp.int32)[None, None, :]
    return (pairs, row_gates, slots)


def block_scores(block_queries, seq_keys, start_row, block_rows, seq_length):
    raw_scores = jnp.einsum(
        "qgrd,kgd->grqk", block_queries, seq_keys, preferred_element_type=jnp.float32
    )
    query_pos = start_row + jnp.arange(block_rows, dtype=jnp.int32)[:, None]
    key_pos = jnp.arange(seq_length, dtype=jnp.int32)[None, :]
    return jnp.where(key_pos <= query_pos, raw_scores * HEAD_DIM ** (-0.5), negative)


def attend_forward(queries, key_rows, value_rows, seq_length, block_rows):
    row_count = queries.shape[0]
    kv_local = key_rows.shape[1]
    repeat_count = queries.shape[1] // kv_local
    seq_count = row_count // seq_length

    def one_sequence(pieces):
        seq_queries, seq_keys, seq_values = pieces
        out_blocks = []
        lse_blocks = []
        for block_index in range(seq_length // block_rows):
            start_row = block_index * block_rows
            block_queries = seq_queries[start_row : start_row + block_rows]
            scores = block_scores(block_queries, seq_keys, start_row, block_rows, seq_length)
            largest = jnp.max(scores, -1, keepdims=True)
            log_total = largest + jnp.log(jnp.sum(jnp.exp(scores - largest), -1, keepdims=True))
            probabilities = jnp.exp(scores - log_total).astype(jnp.bfloat16)
            block_out = jnp.einsum(
                "grqk,kgd->qgrd", probabilities, seq_values, preferred_element_type=jnp.float32
            )
            out_blocks.append(block_out.reshape(block_rows, -1))
            lse_blocks.append(log_total)
        return (jnp.concatenate(out_blocks, 0), jnp.concatenate(lse_blocks, 2))

    attended_values, log_sums = lax.map(
        one_sequence,
        (
            queries.reshape(seq_count, seq_length, kv_local, repeat_count, HEAD_DIM),
            key_rows.reshape(seq_count, seq_length, kv_local, HEAD_DIM),
            value_rows.reshape(seq_count, seq_length, kv_local, HEAD_DIM),
        ),
    )
    return (attended_values.reshape(row_count, -1), log_sums)


def attend_backward(queries, key_rows, value_rows, grad_mixed, log_sums, seq_length, block_rows):
    row_count = queries.shape[0]
    kv_local = key_rows.shape[1]
    repeat_count = queries.shape[1] // kv_local
    seq_count = row_count // seq_length
    scale = HEAD_DIM ** (-0.5)

    def one_sequence(pieces):
        seq_queries, seq_keys, seq_values, seq_grads, seq_sums = pieces
        grad_keys = jnp.zeros((seq_length, kv_local, HEAD_DIM), jnp.float32)
        grad_values = jnp.zeros((seq_length, kv_local, HEAD_DIM), jnp.float32)
        query_blocks = []
        for block_index in range(seq_length // block_rows):
            start_row = block_index * block_rows
            block_queries = seq_queries[start_row : start_row + block_rows]
            block_grads = seq_grads[start_row : start_row + block_rows]
            block_sums = seq_sums[:, :, start_row : start_row + block_rows]
            scores = block_scores(block_queries, seq_keys, start_row, block_rows, seq_length)
            probabilities = jnp.exp(scores - block_sums)
            rounded = probabilities.astype(jnp.bfloat16)
            grad_probs = jnp.einsum(
                "qgrd,kgd->grqk", block_grads, seq_values, preferred_element_type=jnp.float32
            )
            inner = jnp.sum(probabilities * grad_probs, -1, keepdims=True)
            grad_scores = (scale * probabilities * (grad_probs - inner)).astype(jnp.bfloat16)
            query_blocks.append(
                jnp.einsum(
                    "grqk,kgd->qgrd", grad_scores, seq_keys, preferred_element_type=jnp.float32
                )
            )
            grad_keys = grad_keys + jnp.einsum(
                "grqk,qgrd->kgd", grad_scores, block_queries, preferred_element_type=jnp.float32
            )
            grad_values = grad_values + jnp.einsum(
                "grqk,qgrd->kgd", rounded, block_grads, preferred_element_type=jnp.float32
            )
        return (jnp.concatenate(query_blocks, 0), grad_keys, grad_values)

    grad_queries, grad_keys, grad_values = lax.map(
        one_sequence,
        (
            queries.reshape(seq_count, seq_length, kv_local, repeat_count, HEAD_DIM),
            key_rows.reshape(seq_count, seq_length, kv_local, HEAD_DIM),
            value_rows.reshape(seq_count, seq_length, kv_local, HEAD_DIM),
            grad_mixed.reshape(seq_count, seq_length, kv_local, repeat_count, HEAD_DIM),
            log_sums,
        ),
    )
    return (
        grad_queries.reshape(row_count, kv_local * repeat_count, HEAD_DIM),
        grad_keys.reshape(row_count, kv_local, HEAD_DIM),
        grad_values.reshape(row_count, kv_local * HEAD_DIM),
    )


def on_device(
    tokens,
    gain_attn,
    gain_ffn,
    w_query,
    w_key,
    w_value,
    w_out,
    w_gate,
    w_up,
    w_down,
    route_gates,
    routes,
    cotangent,
):
    tensor_size = lax.axis_size("tensor")
    own_rows = tokens.shape[0]
    group_rows = own_rows * tensor_size
    seq_length = min(LEN, group_rows)
    block_rows = min(512, seq_length)
    capacity = group_rows * TOP * 5 // (4 * EXPERTS)
    local_experts = w_gate.shape[0]
    head_count = w_query.shape[1] // HEAD_DIM
    kv_count = w_key.shape[1] // HEAD_DIM
    query_width = w_query.shape[1]
    key_width = w_key.shape[1]
    pre_width = query_width + 2 * key_width
    rows_shard = w_query.shape[0]
    owns_experts = local_experts == lax.axis_size("dp") and 2 * w_gate.shape[2] == D
    cosine, sine_table = rope_tables(group_rows, seq_length)
    attn_full = lax.all_gather(
        jnp.concatenate([w_query, w_key, w_value, w_out.T], 1), "dp", axis=0, tiled=True
    )
    pre_full = attn_full[:, :pre_width]
    out_full = attn_full[:, pre_width:]
    def to_experts(rows):
        if not owns_experts:
            return rows.reshape(local_experts, capacity, D)
        moved = lax.all_to_all(
            rows.reshape(local_experts, capacity, D), "dp", split_axis=0, concat_axis=0, tiled=True
        )
        return moved.reshape(1, local_experts * capacity, D)

    def from_experts(rows):
        if not owns_experts:
            return rows.reshape(-1, D)
        moved = lax.all_to_all(
            rows.reshape(local_experts, capacity, D), "dp", split_axis=0, concat_axis=0, tiled=True
        )
        return moved.reshape(-1, D)

    pairs, row_gates, slots = dispatch(
        routes, route_gates, lax.axis_index("tensor") * local_experts, local_experts, capacity
    )
    slot_rows = slots.reshape(group_rows, -1).astype(jnp.bfloat16)
    gated_rows = (
        jnp.where(slots, row_gates[:, :, None], 0.0).astype(jnp.bfloat16).reshape(group_rows, -1)
    )
    slot_gate = jnp.sum(jnp.where(slots, row_gates[:, :, None], 0.0), 0).reshape(-1)
    grad_full = spread(cotangent)
    grad_slots = jnp.einsum("ts,td->sd", slot_rows, grad_full, preferred_element_type=jnp.float32)
    grad_rows = (slot_gate[:, None] * grad_slots).astype(jnp.bfloat16)
    down_rows = w_down.transpose(0, 2, 1)
    if owns_experts:
        half = rows_shard // 2
        width = w_gate.shape[2]
        moved = lax.all_to_all(
            jnp.concatenate(
                [
                    jnp.concatenate([w_gate, w_up], 2),
                    jnp.concatenate([down_rows[:, :half], down_rows[:, half:]], 2),
                    grad_rows.reshape(local_experts, capacity, D),
                ],
                1,
            ),
            "dp",
            split_axis=0,
            concat_axis=0,
            tiled=True,
        )
        gate_full = moved[:, :rows_shard, :width].reshape(1, D, width)
        up_full = moved[:, :rows_shard, width:].reshape(1, D, width)
        down_moved = moved[:, rows_shard : rows_shard + half]
        down_full = jnp.concatenate(
            [down_moved[:, :, :width], down_moved[:, :, width:]], 1
        ).reshape(1, D, width)
        grad_expert = moved[:, rows_shard + half :].reshape(1, local_experts * capacity, D)
    else:
        expert_full = lax.all_gather(
            jnp.stack([w_gate, w_up, down_rows], 1), "dp", axis=2, tiled=True
        )
        gate_full, up_full, down_full = (expert_full[:, index] for index in range(3))
        grad_expert = to_experts(grad_rows)

    token_values = tokens.astype(jnp.float32)
    normed_own, scaled_attn, factor_attn = normalize(token_values, gain_attn)
    normed = spread(normed_own)
    pre = jnp.dot(normed, pre_full, preferred_element_type=jnp.float32)
    query_pre = pre[:, :query_width]
    key_pre = pre[:, query_width : query_width + key_width]
    value_pre = pre[:, query_width + key_width :]
    queries = rotate(
        query_pre.reshape(group_rows, head_count, HEAD_DIM), cosine, sine_table
    ).astype(jnp.bfloat16)
    key_rows = rotate(key_pre.reshape(group_rows, kv_count, HEAD_DIM), cosine, sine_table).astype(
        jnp.bfloat16
    )
    value_rows = value_pre.reshape(group_rows, kv_count, HEAD_DIM).astype(jnp.bfloat16)
    attended_values, log_sums = attend_forward(
        queries, key_rows, value_rows, seq_length, block_rows
    )
    mixed = attended_values.astype(jnp.bfloat16)
    attended = token_values + sum_rows(
        jnp.einsum("tc,dc->td", mixed, out_full, preferred_element_type=jnp.float32)
    )
    routed_own, scaled_ffn, factor_ffn = normalize(attended, gain_ffn)
    routed = spread(routed_own)
    expert_in = to_experts(
        jnp.einsum("ts,td->sd", slot_rows, routed, preferred_element_type=jnp.float32).astype(
            jnp.bfloat16
        )
    )
    gate_pre = jnp.einsum("ecd,edf->ecf", expert_in, gate_full, preferred_element_type=jnp.float32)
    up_pre = jnp.einsum("ecd,edf->ecf", expert_in, up_full, preferred_element_type=jnp.float32)
    sigmoid_gate = jax.nn.sigmoid(gate_pre)
    silu_gate = gate_pre * sigmoid_gate
    hidden = (silu_gate * up_pre).astype(jnp.bfloat16)
    expert_out = from_experts(
        jnp.einsum("ecf,edf->ecd", hidden, down_full, preferred_element_type=jnp.float32).astype(
            jnp.bfloat16
        )
    )
    grad_hidden = jnp.einsum(
        "ecd,edf->ecf", grad_expert, down_full, preferred_element_type=jnp.float32
    )
    grad_gate_pre = (
        grad_hidden * up_pre * sigmoid_gate * (1.0 + gate_pre * (1.0 - sigmoid_gate))
    ).astype(jnp.bfloat16)
    grad_up_pre = (grad_hidden * silu_gate).astype(jnp.bfloat16)
    grad_expert_in = jnp.einsum(
        "ecf,edf->ecd", grad_gate_pre, gate_full, preferred_element_type=jnp.float32
    )
    grad_expert_in = grad_expert_in + jnp.einsum(
        "ecf,edf->ecd", grad_up_pre, up_full, preferred_element_type=jnp.float32
    )
    routed_slots = from_experts(grad_expert_in.astype(jnp.bfloat16))
    grad_stack = jnp.stack(
        [
            jnp.einsum("ecd,ecf->edf", left, right, preferred_element_type=jnp.float32).astype(
                jnp.bfloat16
            )
            for left, right in (
                (expert_in, grad_gate_pre),
                (expert_in, grad_up_pre),
                (grad_expert, hidden),
            )
        ],
        1,
    )
    if owns_experts:
        grad_shards = lax.all_to_all(
            grad_stack.reshape(3, local_experts, rows_shard, -1).transpose(1, 0, 2, 3),
            "dp",
            split_axis=0,
            concat_axis=0,
            tiled=True,
        )
    else:
        grad_shards = lax.psum_scatter(grad_stack, "dp", scatter_dimension=2, tiled=True)
    grad_shards = grad_shards.astype(jnp.float32)
    grad_gate, grad_up = (grad_shards[:, 0], grad_shards[:, 1])
    grad_down = grad_shards[:, 2].transpose(0, 2, 1)

    routed_part = jnp.dot(slot_rows, routed_slots, preferred_element_type=jnp.float32)
    grad_routed = sum_rows(routed_part)
    combined = jnp.dot(gated_rows, expert_out, preferred_element_type=jnp.float32)
    layer_out = (attended + sum_rows(combined)).astype(jnp.bfloat16)
    gate_grad = jnp.sum(grad_slots * expert_out.astype(jnp.float32), -1)
    row_grads = jnp.sum(
        jnp.where(slots, gate_grad.reshape(1, local_experts, capacity), 0.0), -1
    )
    gate_part = jnp.sum(jnp.where(pairs, row_grads[:, None, :], 0.0), -1)
    grad_gates = lax.psum_scatter(gate_part, "tensor", scatter_dimension=0, tiled=True)

    gain_ffn_part, attended_norm = normalize_back(grad_routed, scaled_ffn, factor_ffn, gain_ffn)
    grad_attended = cotangent.astype(jnp.float32) + attended_norm
    grad_branch = spread(grad_attended.astype(jnp.bfloat16))
    grad_out_w = jnp.einsum("td,tc->dc", grad_branch, mixed, preferred_element_type=jnp.float32)
    grad_mixed = jnp.dot(grad_branch, out_full, preferred_element_type=jnp.float32).astype(
        jnp.bfloat16
    )
    grad_queries, grad_keys, grad_values = attend_backward(
        queries, key_rows, value_rows, grad_mixed, log_sums, seq_length, block_rows
    )
    grad_query_pre = (
        rotate_back(grad_queries, cosine, sine_table).astype(jnp.bfloat16).reshape(group_rows, -1)
    )
    grad_key_pre = (
        rotate_back(grad_keys, cosine, sine_table).astype(jnp.bfloat16).reshape(group_rows, -1)
    )
    grad_pre = jnp.concatenate([grad_query_pre, grad_key_pre, grad_values.astype(jnp.bfloat16)], 1)
    grad_pre_w = jnp.einsum("td,tc->dc", normed, grad_pre, preferred_element_type=jnp.float32)
    grad_normed = sum_rows(
        jnp.einsum("tc,dc->td", grad_pre, pre_full, preferred_element_type=jnp.float32)
    )
    gain_attn_part, tokens_norm = normalize_back(grad_normed, scaled_attn, factor_attn, gain_attn)
    grad_tokens = grad_attended + tokens_norm
    gain_parts = lax.all_gather(
        jnp.stack([gain_attn_part, gain_ffn_part]), ("dp", "tensor"), axis=0, tiled=False
    )
    gain_sums = jnp.sum(gain_parts, 0)
    grad_gain_attn, grad_gain_ffn = (gain_sums[0], gain_sums[1])
    attn_moved = lax.all_to_all(
        jnp.concatenate(
            [grad_pre_w.astype(jnp.bfloat16), grad_out_w.astype(jnp.bfloat16)], 1
        ).reshape(-1, rows_shard, pre_width + query_width),
        "dp",
        split_axis=0,
        concat_axis=0,
        tiled=True,
    )
    attn_shards = jnp.sum(attn_moved.astype(jnp.float32), 0)
    grad_query = attn_shards[:, :query_width]
    grad_key = attn_shards[:, query_width : query_width + key_width]
    grad_value = attn_shards[:, query_width + key_width : pre_width]
    grad_out = attn_shards[:, pre_width:].T
    return (
        layer_out,
        grad_tokens,
        grad_gates,
        grad_gain_attn,
        grad_gain_ffn,
        grad_query,
        grad_key,
        grad_value,
        grad_out,
        grad_gate,
        grad_up,
        grad_down,
    )


def solution(mesh):
    in_specs = (
        P(("dp", "tensor"), None),
        P(),
        P(),
        P("dp", "tensor"),
        P("dp", "tensor"),
        P("dp", "tensor"),
        P("tensor", "dp"),
        P("tensor", "dp", None),
        P("tensor", "dp", None),
        P("tensor", None, "dp"),
        P("dp", None),
        P("dp", None),
        P(("dp", "tensor"), None),
    )
    out_specs = (
        P(("dp", "tensor"), None),
        P(("dp", "tensor"), None),
        P(("dp", "tensor"), None),
        P(),
        P(),
        P("dp", "tensor"),
        P("dp", "tensor"),
        P("dp", "tensor"),
        P("tensor", "dp"),
        P("tensor", "dp", None),
        P("tensor", "dp", None),
        P("tensor", None, "dp"),
    )
    return jax.shard_map(
        on_device, mesh=mesh, in_specs=in_specs, out_specs=out_specs, check_vma=False
    )
```

```python
import jax
import jax.numpy as jnp
from jax import lax
from jax.sharding import PartitionSpec as P

D = 1024
HEAD_DIM = 64
EXPERTS = 32
TOP = 8
LEN = 1024


epsilon = 1e-06
rope_base = 10000.0
negative = -1e30


def rope_tables(count_rows, seq_length):
    positions = (jnp.arange(count_rows, dtype=jnp.int32) % seq_length).astype(jnp.float32)
    freqs = rope_base ** (
        -(jnp.arange(HEAD_DIM // 2, dtype=jnp.int32).astype(jnp.float32) * 2.0 / HEAD_DIM)
    )
    angles = positions[:, None] * freqs[None, :]
    return (
        jnp.concatenate([jnp.cos(angles), jnp.cos(angles)], -1),
        jnp.concatenate([jnp.sin(angles), jnp.sin(angles)], -1),
    )


def rotate(values, cosine, sine_table):
    halfway = values.shape[-1] // 2
    turned = jnp.concatenate([-values[..., halfway:], values[..., :halfway]], -1)
    return values * cosine[:, None, :] + turned * sine_table[:, None, :]


def rotate_back(grads, cosine, sine_table):
    halfway = grads.shape[-1] // 2
    shifted = grads * sine_table[:, None, :]
    reverted = jnp.concatenate([shifted[..., halfway:], -shifted[..., :halfway]], -1)
    return grads * cosine[:, None, :] + reverted


def normalize(values, gain_vector):
    factor = lax.rsqrt(jnp.mean(values * values, -1, keepdims=True) + epsilon)
    scaled = values * factor
    return ((scaled * gain_vector).astype(jnp.bfloat16), scaled, factor)


def normalize_back(grad_normed, scaled, factor, gain_vector):
    grad_scaled = grad_normed * gain_vector
    gain_term = jnp.sum(grad_normed * scaled, 0)
    grad_values = factor * (
        grad_scaled - scaled * jnp.mean(grad_scaled * scaled, -1, keepdims=True)
    )
    return (gain_term, grad_values)


def spread(values):
    return lax.all_gather(values, "tensor", axis=0, tiled=True)


def sum_rows(term):
    size = lax.axis_size("tensor")
    own_rows = term.shape[0] // size
    if size != 2:
        return lax.psum_scatter(term, "tensor", scatter_dimension=0, tiled=True)
    index = lax.axis_index("tensor")
    kept = lax.dynamic_slice_in_dim(term, index * own_rows, own_rows, 0)
    sent = lax.dynamic_slice_in_dim(term, (1 - index) * own_rows, own_rows, 0)
    received = lax.ppermute(sent.astype(jnp.bfloat16), "tensor", [(0, 1), (1, 0)])
    return kept + received.astype(jnp.float32)


def dispatch(route_rows, gate_rows, first_expert, expert_count, capacity):
    rows = route_rows.shape[0]
    experts = first_expert + jnp.arange(expert_count, dtype=jnp.int32)
    pairs = route_rows[:, :, None] == experts[None, None, :]
    named = jnp.any(pairs, 1)
    row_gates = jnp.sum(jnp.where(pairs, gate_rows[:, :, None], 0.0), 1)
    order = jnp.arange(rows, dtype=jnp.int32)
    before = (order[None, :] < order[:, None]).astype(jnp.bfloat16)
    rank = jnp.dot(
        before, named.astype(jnp.bfloat16), preferred_element_type=jnp.float32
    ).astype(jnp.int32)
    rank = jnp.where(named, rank, capacity)
    slots = rank[:, :, None] == jnp.arange(capacity, dtype=jnp.int32)[None, None, :]
    return (pairs, row_gates, slots)


def block_scores(block_queries, seq_keys, start_row, block_rows, seq_length):
    raw_scores = jnp.einsum(
        "qgrd,kgd->grqk", block_queries, seq_keys, preferred_element_type=jnp.float32
    )
    query_pos = start_row + jnp.arange(block_rows, dtype=jnp.int32)[:, None]
    key_pos = jnp.arange(seq_length, dtype=jnp.int32)[None, :]
    return jnp.where(key_pos <= query_pos, raw_scores * HEAD_DIM ** (-0.5), negative)


def attend_forward(queries, key_rows, value_rows, seq_length, block_rows):
    row_count = queries.shape[0]
    kv_local = key_rows.shape[1]
    repeat_count = queries.shape[1] // kv_local
    seq_count = row_count // seq_length

    def one_sequence(pieces):
        seq_queries, seq_keys, seq_values = pieces
        out_blocks = []
        lse_blocks = []
        for block_index in range(seq_length // block_rows):
            start_row = block_index * block_rows
            block_queries = seq_queries[start_row : start_row + block_rows]
            scores = block_scores(block_queries, seq_keys, start_row, block_rows, seq_length)
            largest = jnp.max(scores, -1, keepdims=True)
            log_total = largest + jnp.log(jnp.sum(jnp.exp(scores - largest), -1, keepdims=True))
            probabilities = jnp.exp(scores - log_total).astype(jnp.bfloat16)
            block_out = jnp.einsum(
                "grqk,kgd->qgrd", probabilities, seq_values, preferred_element_type=jnp.float32
            )
            out_blocks.append(block_out.reshape(block_rows, -1))
            lse_blocks.append(log_total)
        return (jnp.concatenate(out_blocks, 0), jnp.concatenate(lse_blocks, 2))

    attended_values, log_sums = lax.map(
        one_sequence,
        (
            queries.reshape(seq_count, seq_length, kv_local, repeat_count, HEAD_DIM),
            key_rows.reshape(seq_count, seq_length, kv_local, HEAD_DIM),
            value_rows.reshape(seq_count, seq_length, kv_local, HEAD_DIM),
        ),
    )
    return (attended_values.reshape(row_count, -1), log_sums)


def attend_backward(queries, key_rows, value_rows, grad_mixed, log_sums, seq_length, block_rows):
    row_count = queries.shape[0]
    kv_local = key_rows.shape[1]
    repeat_count = queries.shape[1] // kv_local
    seq_count = row_count // seq_length
    scale = HEAD_DIM ** (-0.5)

    def one_sequence(pieces):
        seq_queries, seq_keys, seq_values, seq_grads, seq_sums = pieces
        grad_keys = jnp.zeros((seq_length, kv_local, HEAD_DIM), jnp.float32)
        grad_values = jnp.zeros((seq_length, kv_local, HEAD_DIM), jnp.float32)
        query_blocks = []
        for block_index in range(seq_length // block_rows):
            start_row = block_index * block_rows
            block_queries = seq_queries[start_row : start_row + block_rows]
            block_grads = seq_grads[start_row : start_row + block_rows]
            block_sums = seq_sums[:, :, start_row : start_row + block_rows]
            scores = block_scores(block_queries, seq_keys, start_row, block_rows, seq_length)
            probabilities = jnp.exp(scores - block_sums)
            rounded = probabilities.astype(jnp.bfloat16)
            grad_probs = jnp.einsum(
                "qgrd,kgd->grqk", block_grads, seq_values, preferred_element_type=jnp.float32
            )
            inner = jnp.sum(probabilities * grad_probs, -1, keepdims=True)
            grad_scores = (scale * probabilities * (grad_probs - inner)).astype(jnp.bfloat16)
            query_blocks.append(
                jnp.einsum(
                    "grqk,kgd->qgrd", grad_scores, seq_keys, preferred_element_type=jnp.float32
                )
            )
            grad_keys = grad_keys + jnp.einsum(
                "grqk,qgrd->kgd", grad_scores, block_queries, preferred_element_type=jnp.float32
            )
            grad_values = grad_values + jnp.einsum(
                "grqk,qgrd->kgd", rounded, block_grads, preferred_element_type=jnp.float32
            )
        return (jnp.concatenate(query_blocks, 0), grad_keys, grad_values)

    grad_queries, grad_keys, grad_values = lax.map(
        one_sequence,
        (
            queries.reshape(seq_count, seq_length, kv_local, repeat_count, HEAD_DIM),
            key_rows.reshape(seq_count, seq_length, kv_local, HEAD_DIM),
            value_rows.reshape(seq_count, seq_length, kv_local, HEAD_DIM),
            grad_mixed.reshape(seq_count, seq_length, kv_local, repeat_count, HEAD_DIM),
            log_sums,
        ),
    )
    return (
        grad_queries.reshape(row_count, kv_local * repeat_count, HEAD_DIM),
        grad_keys.reshape(row_count, kv_local, HEAD_DIM),
        grad_values.reshape(row_count, kv_local * HEAD_DIM),
    )


def on_device(
    tokens,
    gain_attn,
    gain_ffn,
    w_query,
    w_key,
    w_value,
    w_out,
    w_gate,
    w_up,
    w_down,
    route_gates,
    routes,
    cotangent,
):
    tensor_size = lax.axis_size("tensor")
    own_rows = tokens.shape[0]
    group_rows = own_rows * tensor_size
    seq_length = min(LEN, group_rows)
    block_rows = min(512, seq_length)
    capacity = group_rows * TOP * 5 // (4 * EXPERTS)
    local_experts = w_gate.shape[0]
    head_count = w_query.shape[1] // HEAD_DIM
    kv_count = w_key.shape[1] // HEAD_DIM
    query_width = w_query.shape[1]
    key_width = w_key.shape[1]
    pre_width = query_width + 2 * key_width
    rows_shard = w_query.shape[0]
    owns_experts = local_experts == lax.axis_size("dp") and 2 * w_gate.shape[2] == D
    cosine, sine_table = rope_tables(group_rows, seq_length)
    attn_full = lax.all_gather(
        jnp.concatenate([w_query, w_key, w_value, w_out.T], 1), "dp", axis=0, tiled=True
    )
    def to_experts(rows):
        if not owns_experts:
            return rows.reshape(local_experts, capacity, D)
        moved = lax.all_to_all(
            rows.reshape(local_experts, capacity, D), "dp", split_axis=0, concat_axis=0, tiled=True
        )
        return moved.reshape(1, local_experts * capacity, D)

    def from_experts(rows):
        if not owns_experts:
            return rows.reshape(-1, D)
        moved = lax.all_to_all(
            rows.reshape(local_experts, capacity, D), "dp", split_axis=0, concat_axis=0, tiled=True
        )
        return moved.reshape(-1, D)

    pairs, row_gates, slots = dispatch(
        routes, route_gates, lax.axis_index("tensor") * local_experts, local_experts, capacity
    )
    slot_rows = slots.reshape(group_rows, -1).astype(jnp.bfloat16)
    gated_rows = (
        jnp.where(slots, row_gates[:, :, None], 0.0).astype(jnp.bfloat16).reshape(group_rows, -1)
    )
    slot_gate = jnp.sum(jnp.where(slots, row_gates[:, :, None], 0.0), 0).reshape(-1)
    grad_full = spread(cotangent)
    grad_slots = jnp.einsum("ts,td->sd", slot_rows, grad_full, preferred_element_type=jnp.float32)
    grad_rows = (slot_gate[:, None] * grad_slots).astype(jnp.bfloat16)
    down_rows = w_down.transpose(0, 2, 1)
    token_values = tokens.astype(jnp.float32)
    normed_own, scaled_attn, factor_attn = normalize(token_values, gain_attn)
    normed = spread(normed_own)
    attn_full, normed, grad_rows = lax.optimization_barrier((attn_full, normed, grad_rows))
    pre_full = attn_full[:, :pre_width]
    out_full = attn_full[:, pre_width:]
    if owns_experts:
        half = rows_shard // 2
        width = w_gate.shape[2]
        moved = lax.all_to_all(
            jnp.concatenate(
                [
                    jnp.concatenate([w_gate, w_up], 2),
                    jnp.concatenate([down_rows[:, :half], down_rows[:, half:]], 2),
                    grad_rows.reshape(local_experts, capacity, D),
                ],
                1,
            ),
            "dp",
            split_axis=0,
            concat_axis=0,
            tiled=True,
        )
        gate_full = moved[:, :rows_shard, :width].reshape(1, D, width)
        up_full = moved[:, :rows_shard, width:].reshape(1, D, width)
        down_moved = moved[:, rows_shard : rows_shard + half]
        down_full = jnp.concatenate(
            [down_moved[:, :, :width], down_moved[:, :, width:]], 1
        ).reshape(1, D, width)
        grad_expert = moved[:, rows_shard + half :].reshape(1, local_experts * capacity, D)
    else:
        expert_full = lax.all_gather(
            jnp.stack([w_gate, w_up, down_rows], 1), "dp", axis=2, tiled=True
        )
        gate_full, up_full, down_full = (expert_full[:, index] for index in range(3))
        grad_expert = to_experts(grad_rows)

    pre = jnp.dot(normed, pre_full, preferred_element_type=jnp.float32)
    query_pre = pre[:, :query_width]
    key_pre = pre[:, query_width : query_width + key_width]
    value_pre = pre[:, query_width + key_width :]
    queries = rotate(
        query_pre.reshape(group_rows, head_count, HEAD_DIM), cosine, sine_table
    ).astype(jnp.bfloat16)
    key_rows = rotate(key_pre.reshape(group_rows, kv_count, HEAD_DIM), cosine, sine_table).astype(
        jnp.bfloat16
    )
    value_rows = value_pre.reshape(group_rows, kv_count, HEAD_DIM).astype(jnp.bfloat16)
    attended_values, log_sums = attend_forward(
        queries, key_rows, value_rows, seq_length, block_rows
    )
    mixed = attended_values.astype(jnp.bfloat16)
    attended = token_values + sum_rows(
        jnp.einsum("tc,dc->td", mixed, out_full, preferred_element_type=jnp.float32)
    )
    routed_own, scaled_ffn, factor_ffn = normalize(attended, gain_ffn)
    routed = spread(routed_own)
    expert_in = to_experts(
        jnp.einsum("ts,td->sd", slot_rows, routed, preferred_element_type=jnp.float32).astype(
            jnp.bfloat16
        )
    )
    gate_pre = jnp.einsum("ecd,edf->ecf", expert_in, gate_full, preferred_element_type=jnp.float32)
    up_pre = jnp.einsum("ecd,edf->ecf", expert_in, up_full, preferred_element_type=jnp.float32)
    sigmoid_gate = jax.nn.sigmoid(gate_pre)
    silu_gate = gate_pre * sigmoid_gate
    hidden = (silu_gate * up_pre).astype(jnp.bfloat16)
    expert_rows = jnp.einsum(
        "ecf,edf->ecd", hidden, down_full, preferred_element_type=jnp.float32
    ).astype(jnp.bfloat16)
    grad_hidden = jnp.einsum(
        "ecd,edf->ecf", grad_expert, down_full, preferred_element_type=jnp.float32
    )
    grad_gate_pre = (
        grad_hidden * up_pre * sigmoid_gate * (1.0 + gate_pre * (1.0 - sigmoid_gate))
    ).astype(jnp.bfloat16)
    grad_up_pre = (grad_hidden * silu_gate).astype(jnp.bfloat16)
    grad_expert_in = jnp.einsum(
        "ecf,edf->ecd", grad_gate_pre, gate_full, preferred_element_type=jnp.float32
    )
    grad_expert_in = grad_expert_in + jnp.einsum(
        "ecf,edf->ecd", grad_up_pre, up_full, preferred_element_type=jnp.float32
    )
    routed_slots = from_experts(grad_expert_in.astype(jnp.bfloat16))
    grad_gate_w, grad_up_w, grad_down_w = (
        jnp.einsum("ecd,ecf->edf", left, right, preferred_element_type=jnp.float32).astype(
            jnp.bfloat16
        )
        for left, right in (
            (expert_in, grad_gate_pre),
            (expert_in, grad_up_pre),
            (grad_expert, hidden),
        )
    )
    if owns_experts:
        grad_gate_w, grad_up_w, grad_down_w = (
            value.reshape(local_experts, rows_shard, width)
            for value in (grad_gate_w, grad_up_w, grad_down_w)
        )
        moved = lax.all_to_all(
            jnp.concatenate(
                [
                    jnp.concatenate([grad_gate_w, grad_up_w], 2),
                    jnp.concatenate([grad_down_w[:, :half], grad_down_w[:, half:]], 2),
                    expert_rows.reshape(local_experts, capacity, D),
                ],
                1,
            ),
            "dp",
            split_axis=0,
            concat_axis=0,
            tiled=True,
        )
    else:
        grad_gate, grad_up, grad_down = (
            lax.psum_scatter(value, "dp", scatter_dimension=1, tiled=True).astype(jnp.float32)
            for value in (grad_gate_w, grad_up_w, grad_down_w)
        )
        expert_out = expert_rows.reshape(-1, D)
    routed_part = jnp.dot(slot_rows, routed_slots, preferred_element_type=jnp.float32)
    grad_routed = sum_rows(routed_part)
    gain_ffn_part, attended_norm = normalize_back(grad_routed, scaled_ffn, factor_ffn, gain_ffn)
    grad_attended = cotangent.astype(jnp.float32) + attended_norm
    grad_branch = spread(grad_attended.astype(jnp.bfloat16))
    grad_out_w = jnp.einsum("td,tc->dc", grad_branch, mixed, preferred_element_type=jnp.float32)
    grad_mixed = jnp.dot(grad_branch, out_full, preferred_element_type=jnp.float32).astype(
        jnp.bfloat16
    )
    grad_queries, grad_keys, grad_values = attend_backward(
        queries, key_rows, value_rows, grad_mixed, log_sums, seq_length, block_rows
    )
    grad_query_pre = (
        rotate_back(grad_queries, cosine, sine_table).astype(jnp.bfloat16).reshape(group_rows, -1)
    )
    grad_key_pre = (
        rotate_back(grad_keys, cosine, sine_table).astype(jnp.bfloat16).reshape(group_rows, -1)
    )
    grad_pre = jnp.concatenate([grad_query_pre, grad_key_pre, grad_values.astype(jnp.bfloat16)], 1)
    if owns_experts:
        moved, grad_pre = lax.optimization_barrier((moved, grad_pre))
        grad_gate = moved[:, :rows_shard, :width].astype(jnp.float32)
        grad_up = moved[:, :rows_shard, width:].astype(jnp.float32)
        down_moved = moved[:, rows_shard : rows_shard + half].astype(jnp.float32)
        grad_down = jnp.concatenate([down_moved[:, :, :width], down_moved[:, :, width:]], 1)
        expert_out = moved[:, rows_shard + half :].reshape(-1, D)
    grad_down = grad_down.transpose(0, 2, 1)
    combined = jnp.dot(gated_rows, expert_out, preferred_element_type=jnp.float32)
    layer_out = (attended + sum_rows(combined)).astype(jnp.bfloat16)
    gate_grad = jnp.sum(grad_slots * expert_out.astype(jnp.float32), -1)
    row_grads = jnp.sum(
        jnp.where(slots, gate_grad.reshape(1, local_experts, capacity), 0.0), -1
    )
    gate_part = jnp.sum(jnp.where(pairs, row_grads[:, None, :], 0.0), -1)
    grad_gates = lax.psum_scatter(gate_part, "tensor", scatter_dimension=0, tiled=True)
    grad_pre_w = jnp.einsum("td,tc->dc", normed, grad_pre, preferred_element_type=jnp.float32)
    grad_normed = sum_rows(
        jnp.einsum("tc,dc->td", grad_pre, pre_full, preferred_element_type=jnp.float32)
    )
    gain_attn_part, tokens_norm = normalize_back(grad_normed, scaled_attn, factor_attn, gain_attn)
    grad_tokens = grad_attended + tokens_norm
    grad_gain_attn, grad_gain_ffn = lax.psum((gain_attn_part, gain_ffn_part), ("dp", "tensor"))
    attn_moved = lax.all_to_all(
        jnp.concatenate(
            [grad_pre_w.astype(jnp.bfloat16), grad_out_w.astype(jnp.bfloat16)], 1
        ).reshape(-1, rows_shard, pre_width + query_width),
        "dp",
        split_axis=0,
        concat_axis=0,
        tiled=True,
    )
    attn_shards = jnp.sum(attn_moved.astype(jnp.float32), 0)
    grad_query = attn_shards[:, :query_width]
    grad_key = attn_shards[:, query_width : query_width + key_width]
    grad_value = attn_shards[:, query_width + key_width : pre_width]
    grad_out = attn_shards[:, pre_width:].T
    return (
        layer_out,
        grad_tokens,
        grad_gates,
        grad_gain_attn,
        grad_gain_ffn,
        grad_query,
        grad_key,
        grad_value,
        grad_out,
        grad_gate,
        grad_up,
        grad_down,
    )


def solution(mesh):
    in_specs = (
        P(("dp", "tensor"), None),
        P(),
        P(),
        P("dp", "tensor"),
        P("dp", "tensor"),
        P("dp", "tensor"),
        P("tensor", "dp"),
        P("tensor", "dp", None),
        P("tensor", "dp", None),
        P("tensor", None, "dp"),
        P("dp", None),
        P("dp", None),
        P(("dp", "tensor"), None),
    )
    out_specs = (
        P(("dp", "tensor"), None),
        P(("dp", "tensor"), None),
        P(("dp", "tensor"), None),
        P(),
        P(),
        P("dp", "tensor"),
        P("dp", "tensor"),
        P("dp", "tensor"),
        P("tensor", "dp"),
        P("tensor", "dp", None),
        P("tensor", "dp", None),
        P("tensor", None, "dp"),
    )
    return jax.shard_map(
        on_device, mesh=mesh, in_specs=in_specs, out_specs=out_specs, check_vma=False
    )
```
